32 devices in a mesh: row: 4 (over y, x), col: 2 (over core), depth: 4 (over z).
Axes of the slice: x: 2, y: 2, z: 4, core: 2. Of those that a mesh axis runs over, the one named last changes fastest.
Arguments:
- inputs: bfloat16 [512, 12288], P(('row', 'col'), 'depth'), may hold values from -90 to 90
- ln_gain: float32 [12288], P('depth'), may hold values from 0.25 to 1.75
- ln_shift: float32 [12288], P('depth'), may hold values from -3 to 3
- w_in: bfloat16 [12288, 24576], P('depth', ('row', 'col')), may hold values from -0.0546875 to 0.0546875
- b_in: float32 [24576], P(('row', 'col')), may hold values from -3 to 3
- w_out: bfloat16 [24576, 12288], P(('row', 'col'), 'depth'), may hold values from -0.0390625 to 0.0390625
- b_out: float32 [12288], P('depth'), may hold values from -3 to 3
- cotangent: bfloat16 [512, 12288], P(('row', 'col'), 'depth'), may hold values from -29 to 29
Outputs:
- output: bfloat16 [512, 12288], P(('row', 'col'), 'depth')
- grad_inputs: bfloat16 [512, 12288], P(('row', 'col'), 'depth')
- grad_w_in: bfloat16 [12288, 24576], P('depth', ('row', 'col'))
- grad_b_in: float32 [24576], P(('row', 'col'))
- grad_w_out: bfloat16 [24576, 12288], P(('row', 'col'), 'depth')
- grad_b_out: float32 [12288], P('depth')
- grad_gain: float32 [12288], P('depth')
- grad_shift: float32 [12288], P('depth')
The draws below stay inside these ranges and needn't reach their ends.
All inputs are finite; a program needn't handle non-finite values.
Results may differ from the reference program's by a relative error of at most 0.0062.
Values may be sent and summed in bfloat16 or wider, within the bound.
A program may use at most 192 MiB of HBM per device.

```python
from functools import partial
import jax
import jax.numpy as jnp
from jax import lax

D = 12288
FF = 24576
TOKENS = 512


def draw_inputs(key, part):
    key = jax.random.fold_in(key, 5)
    key_rows = jax.random.fold_in(key, 0)
    key_cols = jax.random.fold_in(key, 1)
    key_base = jax.random.fold_in(key, 2)
    key_offset = jax.random.fold_in(key, 4)
    key_sign = jax.random.fold_in(key, 5)
    row_scale = jnp.exp(jax.random.uniform(key_rows, (TOKENS, 1)) * jnp.log(10.0))
    col_place = jnp.arange(D, dtype=jnp.float32)[None, :] / D
    col_scale = jnp.exp(col_place * jnp.log(3.0) + jax.random.uniform(key_cols, (1, D)) * jnp.log(3.0))
    row_offset = jax.random.uniform(key_offset, (TOKENS, 1), minval=0.5, maxval=1.5)
    row_sign = jax.random.bernoulli(key_sign, 0.5, (TOKENS, 1)).astype(jnp.float32) * 2.0 - 1.0
    offset_rise = jnp.exp(col_place * jnp.log(5.0))
    base_draw = jnp.clip(jax.random.normal(key_base, (TOKENS, D)), -6.0, 6.0)
    shifted = base_draw * row_scale * col_scale / 6.0 + 0.4 * row_offset * row_sign * offset_rise
    return jnp.clip(shifted, -90.0, 90.0).astype(jnp.bfloat16)


def draw_cotangent(key, part):
    key = jax.random.fold_in(key, 9)
    key_rows, key_cols, key_base = jax.random.split(key, 3)
    row_place = jnp.arange(TOKENS, dtype=jnp.float32)[:, None] / TOKENS
    row_scale = jnp.exp(row_place * jnp.log(3.0) + jax.random.uniform(key_rows, (TOKENS, 1)) * jnp.log(2.0))
    col_scale = jnp.exp(jax.random.uniform(key_cols, (1, D)) * jnp.log(2.0))
    base_draw = jnp.clip(jax.random.normal(key_base, (TOKENS, D)), -6.0, 6.0)
    return (base_draw * row_scale * col_scale * 0.4).astype(jnp.bfloat16)


def steps_of(own_key, dims, shards, low, largest):
    level, own = 1.0, jax.random.fold_in(own_key, 6)
    for axis_at, shards_of in shards:
        heights = jnp.exp(jax.random.uniform(jax.random.fold_in(own, axis_at), (shards_of,), jnp.float32, low / len(shards), largest / len(shards)))
        level = level * jnp.repeat(heights, dims[axis_at] // shards_of).reshape([-1 if axis == axis_at else 1 for axis in range(len(dims))])
    return level


def bell_draw(key, shape, deviation, limit, cuts=(), kind=jnp.bfloat16):
    values = deviation * jax.random.normal(key, shape, jnp.float32)
    if cuts:
        values = values * steps_of(key, shape, cuts, -0.22, 0.18)
    return jnp.clip(values, -limit, limit).astype(kind)


def setup_inputs(seed: int = 0) -> dict:
    keys = jax.random.split(jax.random.key(seed), 9)
    inputs = draw_inputs(jax.random.fold_in(keys[8], 71), 0)
    ln_gain = jnp.clip(1.0 + 0.15 * jax.random.normal(keys[1], (D,), jnp.float32), 0.25, 1.75)
    ln_shift = bell_draw(keys[2], (D,), 0.5, 3.0, ((0, 4),), jnp.float32)
    w_in = bell_draw(keys[3], (D, FF), D ** -0.5, 0.0546875, ((0, 4), (1, 8)))
    b_in = bell_draw(keys[4], (FF,), 0.5, 3.0, ((0, 8),), jnp.float32)
    w_out = bell_draw(keys[5], (FF, D), FF ** -0.5, 0.0390625, ((0, 8), (1, 4)))
    b_out = bell_draw(keys[6], (D,), 0.5, 3.0, ((0, 4),), jnp.float32)
    cotangent = draw_cotangent(jax.random.fold_in(keys[8], 71), 0)
    return {"inputs": inputs, "ln_gain": ln_gain, "ln_shift": ln_shift, "w_in": w_in, "b_in": b_in, "w_out": w_out, "b_out": b_out, "cotangent": cotangent}


def gelu_back(pre_act, upstream):
    return jax.vjp(partial(jax.nn.gelu, approximate=True), pre_act)[1](upstream)[0]

def reference(inputs, ln_gain, ln_shift, w_in, b_in, w_out, b_out, cotangent):
    wide_in = inputs.astype(jnp.float32)
    row_mean = lax.optimization_barrier(jnp.mean(wide_in, axis=1, keepdims=True))
    centred = wide_in - row_mean
    row_var = lax.optimization_barrier(jnp.mean(centred * centred, axis=1, keepdims=True))
    inv_std = 1.0 / jnp.sqrt(row_var + 1e-05)
    normed = centred * inv_std
    hidden_in = (normed * ln_gain + ln_shift).astype(jnp.bfloat16)
    pre_act = jnp.dot(hidden_in, w_in, preferred_element_type=jnp.float32) + b_in
    activated = jax.nn.gelu(pre_act, approximate=True).astype(jnp.bfloat16)
    projected = jnp.dot(activated, w_out, preferred_element_type=jnp.float32) + b_out
    output = (wide_in + projected).astype(jnp.bfloat16)
    act_grad = jnp.dot(cotangent, w_out.T, preferred_element_type=jnp.float32)
    pre_grad = gelu_back(pre_act, act_grad).astype(jnp.bfloat16)
    grad_w_out = jnp.dot(activated.T, cotangent, preferred_element_type=jnp.float32).astype(jnp.bfloat16)
    grad_b_out = lax.optimization_barrier(jnp.sum(cotangent.astype(jnp.float32), axis=0))
    grad_w_in = jnp.dot(hidden_in.T, pre_grad, preferred_element_type=jnp.float32).astype(jnp.bfloat16)
    grad_b_in = lax.optimization_barrier(jnp.sum(pre_grad.astype(jnp.float32), axis=0))
    norm_grad = jnp.dot(pre_grad, w_in.T, preferred_element_type=jnp.float32)
    grad_gain = lax.optimization_barrier(jnp.sum(norm_grad * normed, axis=0))
    grad_shift = lax.optimization_barrier(jnp.sum(norm_grad, axis=0))
    scaled_grad = norm_grad * ln_gain
    first_mean = lax.optimization_barrier(jnp.mean(scaled_grad, axis=1, keepdims=True))
    second_mean = lax.optimization_barrier(jnp.mean(scaled_grad * normed, axis=1, keepdims=True))
    grad_inputs = (cotangent.astype(jnp.float32) + inv_std * (scaled_grad - first_mean - normed * second_mean)).astype(jnp.bfloat16)
    return (output, grad_inputs, grad_w_in, grad_b_in, grad_w_out, grad_b_out, grad_gain, grad_shift)
```

```python
from functools import partial

import jax
import jax.numpy as jnp
from jax import lax
from jax.experimental import pallas as pl
from jax.experimental.pallas import tpu as pltpu
from jax.sharding import PartitionSpec as P

CHUNK = 256
HALVES = 2
SLOTS = 2
LAG = 1
MESH = pl.DeviceIdType.MESH


def gelu_both(pre, upstream):
    root = 0.7978845608028654
    square = pre * pre
    tanh = jnp.tanh(root * pre * (1.0 + 0.044715 * square))
    half = 0.5 * (1.0 + tanh)
    slope = half + 0.5 * pre * (1.0 - tanh * tanh) * (root * (1.0 + 0.134145 * square))
    return pre * half, upstream * slope


def contract_rows(left, right):
    return lax.dot_general(
        left, right, (((0,), (0,)), ((), ())), preferred_element_type=jnp.float32
    )


def contract_cols(left, right):
    return lax.dot_general(
        left, right, (((1,), (1,)), ((), ())), preferred_element_type=jnp.float32
    )


def line_kernel(
    n,
    hidden_hbm,
    grad_hbm,
    w_in,
    w_out,
    b_in,
    active_hbm,
    pre_grad_hbm,
    proj_hbm,
    norm_hbm,
    bias_ref,
    hidden,
    grad,
    own,
    from_left,
    from_right,
    to_right,
    to_left,
    proj,
    norm,
    early_in,
    early_out,
    late_in,
    late_out,
    result,
    load_sem,
    early_sem,
    late_sem,
    result_sem,
    send_right_sem,
    send_left_sem,
    recv_left_sem,
    recv_right_sem,
):
    rows, width = hidden.shape
    chunks = w_in.shape[1] // CHUNK
    sub = rows // HALVES
    me = lax.axis_index("depth")
    has_left, has_right = me > 0, me < n - 1
    left, right = jnp.maximum(me - 1, 0), jnp.minimum(me + 1, n - 1)
    tail = LAG * (n - 1)

    load_hidden = pltpu.make_async_copy(hidden_hbm, hidden, load_sem.at[0])
    load_grad = pltpu.make_async_copy(grad_hbm, grad, load_sem.at[1])
    load_grad.start()
    load_hidden.start()

    def columns(chunk):
        return pl.ds(pl.multiple_of(chunk * CHUNK, CHUNK), CHUNK)

    def weight_loads(chunk, to_in, to_out, sem):
        slot = lax.rem(chunk, 2)
        return (
            pltpu.make_async_copy(w_in.at[:, columns(chunk)], to_in.at[slot], sem.at[slot, 0]),
            pltpu.make_async_copy(w_out.at[columns(chunk), :], to_out.at[slot], sem.at[slot, 1]),
        )

    def start_early(chunk):
        for copy in weight_loads(chunk, early_in, early_out, early_sem):
            copy.start()

    def start_late(chunk):
        for copy in weight_loads(chunk, late_in, late_out, late_sem):
            copy.start()

    start_early(0)
    start_late(0)

    barrier = pltpu.get_barrier_semaphore()

    @pl.when(has_left)
    def _():
        pl.semaphore_signal(barrier, inc=1, device_id={"depth": left}, device_id_type=MESH)

    @pl.when(has_right)
    def _():
        pl.semaphore_signal(barrier, inc=1, device_id={"depth": right}, device_id_type=MESH)

    pl.semaphore_wait(barrier, has_left.astype(jnp.int32) + has_right.astype(jnp.int32))

    proj[...] = jnp.zeros_like(proj)
    norm[...] = jnp.zeros_like(norm)
    load_grad.wait()
    load_hidden.wait()

    def right_copy(chunk, kind, half):
        slot = lax.rem(chunk, SLOTS)
        return pltpu.make_async_remote_copy(
            src_ref=to_right.at[slot, kind, half],
            dst_ref=from_left.at[chunk, kind, half],
            send_sem=send_right_sem.at[slot, kind, half],
            recv_sem=recv_left_sem.at[chunk, kind, half],
            device_id={"depth": right},
            device_id_type=MESH,
        )

    def left_copy(chunk, kind, half):
        slot = lax.rem(chunk, SLOTS)
        return pltpu.make_async_remote_copy(
            src_ref=to_left.at[slot, kind, half],
            dst_ref=from_right.at[chunk, kind, half],
            send_sem=send_left_sem.at[slot, kind, half],
            recv_sem=recv_right_sem.at[chunk, kind, half],
            device_id={"depth": left},
            device_id_type=MESH,
        )

    def pass_on(chunk, kind, half, copy, incoming, outgoing, has_source, has_target):
        slot = lax.rem(chunk, SLOTS)

        @pl.when(has_source)
        def _():
            copy(chunk, kind, half).wait_recv()

        @pl.when(has_target)
        def _():
            @pl.when(chunk >= SLOTS)
            def _():
                copy(chunk - SLOTS, kind, half).wait_send()

            @pl.when(has_source)
            def _():
                outgoing[slot, kind, half] = (
                    own[chunk, kind, half] + incoming[chunk, kind, half].astype(jnp.float32)
                ).astype(jnp.bfloat16)

            @pl.when(jnp.logical_not(has_source))
            def _():
                outgoing[slot, kind, half] = own[chunk, kind, half].astype(jnp.bfloat16)

            copy(chunk, kind, half).start()

    def result_copies(chunk):
        slot = lax.rem(chunk, 2)
        return (
            pltpu.make_async_copy(
                result.at[slot, 0], active_hbm.at[:, columns(chunk)], result_sem.at[slot, 0]
            ),
            pltpu.make_async_copy(
                result.at[slot, 1], pre_grad_hbm.at[:, columns(chunk)], result_sem.at[slot, 1]
            ),
        )

    @pl.loop(0, chunks + tail)
    def _(step):
        @pl.when(step < chunks)
        def _():
            @pl.when(step + 1 < chunks)
            def _():
                start_early(step + 1)

            for copy in weight_loads(step, early_in, early_out, early_sem):
                copy.wait()
            slot = lax.rem(step, 2)
            for half in range(HALVES):
                own[step, 0, half] = contract_cols(
                    grad[half * sub : (half + 1) * sub, :], early_out[slot]
                )
            for half in range(HALVES):
                own[step, 1, half] = jnp.dot(
                    hidden[half * sub : (half + 1) * sub, :],
                    early_in[slot],
                    preferred_element_type=jnp.float32,
                )

        going_right = step - LAG * me
        going_left = step - LAG * (n - 1 - me)
        for kind in range(2):
            for half in range(HALVES):

                @pl.when(jnp.logical_and(going_right >= 0, going_right < chunks))
                def _():
                    pass_on(
                        going_right, kind, half, right_copy, from_left, to_right, has_left, has_right
                    )

                @pl.when(jnp.logical_and(going_left >= 0, going_left < chunks))
                def _():
                    pass_on(
                        going_left, kind, half, left_copy, from_right, to_left, has_right, has_left
                    )

        done = step - tail

        @pl.when(done >= 0)
        def _():
            slot = lax.rem(done, 2)

            @pl.when(done + 1 < chunks)
            def _():
                start_late(done + 1)

            @pl.when(done >= 2)
            def _():
                for copy in result_copies(done - 2):
                    copy.wait()

            for kind in range(2):
                for half in range(HALVES):

                    @pl.when(has_left)
                    def _():
                        own[done, kind, half] += from_left[done, kind, half].astype(jnp.float32)

                    @pl.when(has_right)
                    def _():
                        own[done, kind, half] += from_right[done, kind, half].astype(jnp.float32)

            bias = b_in[:, columns(done)]
            bias_grad = jnp.zeros((1, CHUNK), jnp.float32)
            for half in range(HALVES):
                active, pre_grad = gelu_both(own[done, 1, half] + bias, own[done, 0, half])
                pre_grad = pre_grad.astype(jnp.bfloat16)
                result[slot, 0, half * sub : (half + 1) * sub, :] = active.astype(jnp.bfloat16)
                result[slot, 1, half * sub : (half + 1) * sub, :] = pre_grad
                bias_grad += jnp.sum(pre_grad.astype(jnp.float32), axis=0, keepdims=True)
            bias_ref[:, columns(done)] = bias_grad
            for copy in result_copies(done):
                copy.start()
            for copy in weight_loads(done, late_in, late_out, late_sem):
                copy.wait()

            block = width // 2
            for part in range(2):
                span = slice(part * block, (part + 1) * block)
                proj[:, span] += jnp.dot(
                    result[slot, 0], late_out[slot, :, span], preferred_element_type=jnp.float32
                )
            for part in range(2):
                span = slice(part * block, (part + 1) * block)
                norm[:, span] += contract_cols(result[slot, 1], late_in[slot, span, :])

    hidden[...] = proj[...].astype(jnp.bfloat16)
    grad[...] = norm[...].astype(jnp.bfloat16)
    store_proj = pltpu.make_async_copy(hidden, proj_hbm, load_sem.at[0])
    store_norm = pltpu.make_async_copy(grad, norm_hbm, load_sem.at[1])
    store_proj.start()
    store_norm.start()
    for chunk in range(max(0, chunks - 2), chunks):
        for copy in result_copies(chunk):
            copy.wait()
    for chunk in range(max(0, chunks - SLOTS), chunks):
        for kind in range(2):
            for half in range(HALVES):

                @pl.when(has_right)
                def _():
                    right_copy(chunk, kind, half).wait_send()

                @pl.when(has_left)
                def _():
                    left_copy(chunk, kind, half).wait_send()

    store_proj.wait()
    store_norm.wait()


def line_call(n, hidden_all, grad_all, w_in, w_out, b_in):
    rows, width = hidden_all.shape
    local = w_in.shape[1]
    chunks = local // CHUNK
    sub = rows // HALVES
    anywhere = pl.BlockSpec(memory_space=pl.ANY)
    vmem = pl.BlockSpec(memory_space=pltpu.VMEM)
    bf16, f32 = jnp.bfloat16, jnp.float32
    parts = (2, HALVES)
    return pl.pallas_call(
        partial(line_kernel, n),
        out_shape=(
            jax.ShapeDtypeStruct((rows, local), bf16),
            jax.ShapeDtypeStruct((rows, local), bf16),
            jax.ShapeDtypeStruct((rows, width), bf16),
            jax.ShapeDtypeStruct((rows, width), bf16),
            jax.ShapeDtypeStruct((1, local), f32),
        ),
        in_specs=[anywhere] * 4 + [vmem],
        out_specs=(anywhere,) * 4 + (vmem,),
        scratch_shapes=[
            pltpu.VMEM((rows, width), bf16),
            pltpu.VMEM((rows, width), bf16),
            pltpu.VMEM((chunks, *parts, sub, CHUNK), f32),
            pltpu.VMEM((chunks, *parts, sub, CHUNK), bf16),
            pltpu.VMEM((chunks, *parts, sub, CHUNK), bf16),
            pltpu.VMEM((SLOTS, *parts, sub, CHUNK), bf16),
            pltpu.VMEM((SLOTS, *parts, sub, CHUNK), bf16),
            pltpu.VMEM((rows, width), f32),
            pltpu.VMEM((rows, width), f32),
            pltpu.VMEM((2, width, CHUNK), bf16),
            pltpu.VMEM((2, CHUNK, width), bf16),
            pltpu.VMEM((2, width, CHUNK), bf16),
            pltpu.VMEM((2, CHUNK, width), bf16),
            pltpu.VMEM((2, 2, rows, CHUNK), bf16),
            pltpu.SemaphoreType.DMA((2,)),
            pltpu.SemaphoreType.DMA((2, 2)),
            pltpu.SemaphoreType.DMA((2, 2)),
            pltpu.SemaphoreType.DMA((2, 2)),
            pltpu.SemaphoreType.DMA((SLOTS, *parts)),
            pltpu.SemaphoreType.DMA((SLOTS, *parts)),
            pltpu.SemaphoreType.DMA((chunks, *parts)),
            pltpu.SemaphoreType.DMA((chunks, *parts)),
        ],
        compiler_params=pltpu.CompilerParams(
            collective_id=0, has_side_effects=True, vmem_limit_bytes=62 * 2**20
        ),
        cost_estimate=pl.CostEstimate(
            flops=8 * rows * width * local,
            bytes_accessed=8 * width * local + 12 * rows * width,
            transcendentals=rows * local,
        ),
    )(hidden_all, grad_all, w_in, w_out, b_in)


def per_device(n, inputs, ln_gain, ln_shift, w_in, b_in, w_out, b_out, cotangent):
    width = inputs.shape[1]
    grad_all = lax.all_gather(cotangent, ("row", "col"), axis=0, tiled=True)
    wide_in = inputs.astype(jnp.float32)
    part_mean = jnp.mean(wide_in, axis=1, keepdims=True)
    part_square = jnp.sum((wide_in - part_mean) ** 2, axis=1, keepdims=True)
    stats = lax.all_gather(jnp.concatenate([part_mean, part_square], axis=1), "depth", axis=0)
    row_mean = jnp.mean(stats[:, :, :1], axis=0)
    row_var = (
        jnp.sum(stats[:, :, 1:], axis=0)
        + width * jnp.sum((stats[:, :, :1] - row_mean[None]) ** 2, axis=0)
    ) / (n * width)
    inv_std = 1.0 / jnp.sqrt(row_var + 1e-05)
    normed = (wide_in - row_mean) * inv_std
    hidden_in = (normed * ln_gain + ln_shift).astype(jnp.bfloat16)
    hidden_all = lax.all_gather(hidden_in, ("row", "col"), axis=0, tiled=True)
    active_all, pre_grad_all, proj_part, norm_part, bias_part = line_call(
        n, hidden_all, grad_all, w_in, w_out, b_in.reshape(1, -1)
    )
    projected = (
        lax.psum_scatter(proj_part, ("row", "col"), scatter_dimension=0, tiled=True).astype(
            jnp.float32
        )
        + b_out
    )
    output = (wide_in + projected).astype(jnp.bfloat16)
    norm_grad = lax.psum_scatter(
        norm_part, ("row", "col"), scatter_dimension=0, tiled=True
    ).astype(jnp.float32)
    grad_w_out = contract_rows(active_all, grad_all).astype(jnp.bfloat16)
    grad_w_in = contract_rows(hidden_all, pre_grad_all).astype(jnp.bfloat16)
    scaled_grad = norm_grad * ln_gain
    first_total, second_total, grad_b_in = lax.psum(
        (
            jnp.sum(scaled_grad, axis=1, keepdims=True),
            jnp.sum(scaled_grad * normed, axis=1, keepdims=True),
            bias_part[0] / n,
        ),
        "depth",
    )
    features = n * width
    grad_inputs = (
        cotangent.astype(jnp.float32)
        + inv_std * (scaled_grad - first_total / features - normed * (second_total / features))
    ).astype(jnp.bfloat16)
    grad_b_out, grad_gain, grad_shift = lax.psum(
        (
            jnp.sum(cotangent.astype(jnp.float32), axis=0),
            jnp.sum(norm_grad * normed, axis=0),
            jnp.sum(norm_grad, axis=0),
        ),
        ("row", "col"),
    )
    return (
        output,
        grad_inputs,
        grad_w_in,
        grad_b_in,
        grad_w_out,
        grad_b_out,
        grad_gain,
        grad_shift,
    )


def solution(mesh):
    return jax.shard_map(
        partial(per_device, mesh.shape["depth"]),
        mesh=mesh,
        in_specs=(
            P(("row", "col"), "depth"),
            P("depth"),
            P("depth"),
            P("depth", ("row", "col")),
            P(("row", "col")),
            P(("row", "col"), "depth"),
            P("depth"),
            P(("row", "col"), "depth"),
        ),
        out_specs=(
            P(("row", "col"), "depth"),
            P(("row", "col"), "depth"),
            P("depth", ("row", "col")),
            P(("row", "col")),
            P(("row", "col"), "depth"),
            P("depth"),
            P("depth"),
            P("depth"),
        ),
        check_vma=False,
    )
```

```python
from functools import partial

import jax
import jax.numpy as jnp
from jax import lax
from jax.experimental import pallas as pl
from jax.experimental.pallas import tpu as pltpu
from jax.sharding import PartitionSpec as P

CHUNK = 256
HALVES = 2
SLOTS = 2
LAG = 1
MESH = pl.DeviceIdType.MESH


def gelu_both(pre, upstream):
    root = 0.7978845608028654
    square = pre * pre
    tanh = jnp.tanh(root * pre * (1.0 + 0.044715 * square))
    half = 0.5 * (1.0 + tanh)
    slope = half + 0.5 * pre * (1.0 - tanh * tanh) * (root * (1.0 + 0.134145 * square))
    return pre * half, upstream * slope


def contract_rows(left, right):
    return lax.dot_general(
        left, right, (((0,), (0,)), ((), ())), preferred_element_type=jnp.float32
    )


def contract_cols(left, right):
    return lax.dot_general(
        left, right, (((1,), (1,)), ((), ())), preferred_element_type=jnp.float32
    )


def line_kernel(
    n,
    row_size,
    col_size,
    hidden_hbm,
    grad_hbm,
    w_in,
    w_out,
    b_in,
    b_out,
    ln_gain,
    inputs,
    cotangent,
    normed,
    inv_std,
    active_hbm,
    pre_grad_hbm,
    output_ref,
    grad_inputs_ref,
    bias_ref,
    sums_ref,
    hidden,
    grad,
    own,
    from_left,
    from_right,
    to_right,
    to_left,
    proj,
    norm,
    early_in,
    early_out,
    late_in,
    late_out,
    result,
    load_sem,
    early_sem,
    late_sem,
    result_sem,
    send_right_sem,
    send_left_sem,
    recv_left_sem,
    recv_right_sem,
    twin_recv,
    chip_recv,
    stats_send,
    stats_recv,
    bias_send,
    bias_recv,
    sums_send,
    sums_recv,
    twin_sems,
    chip_sems,
    stats_sems,
    bias_sems,
    sums_sems,
):
    rows, width = hidden.shape
    chunks = w_in.shape[1] // CHUNK
    sub = rows // HALVES
    me = lax.axis_index("depth")
    row, col = lax.axis_index("row"), lax.axis_index("col")
    group = row_size * col_size
    chips = group // 2
    per_row = col_size // 2
    core = lax.rem(col, 2)
    place = row * col_size + col
    chip = row * per_row + col // 2
    block_rows = rows // group
    has_left, has_right = me > 0, me < n - 1
    left, right = jnp.maximum(me - 1, 0), jnp.minimum(me + 1, n - 1)
    tail = LAG * (n - 1)
    ring = own.shape[0]

    load_hidden = pltpu.make_async_copy(hidden_hbm, hidden, load_sem.at[0])
    load_grad = pltpu.make_async_copy(grad_hbm, grad, load_sem.at[1])
    load_grad.start()
    load_hidden.start()

    def columns(chunk):
        return pl.ds(pl.multiple_of(chunk * CHUNK, CHUNK), CHUNK)

    def weight_loads(chunk, to_in, to_out, sem):
        slot = lax.rem(chunk, 2)
        return (
            pltpu.make_async_copy(w_in.at[:, columns(chunk)], to_in.at[slot], sem.at[slot, 0]),
            pltpu.make_async_copy(w_out.at[columns(chunk), :], to_out.at[slot], sem.at[slot, 1]),
        )

    def start_early(chunk):
        for copy in weight_loads(chunk, early_in, early_out, early_sem):
            copy.start()

    def start_late(chunk):
        for copy in weight_loads(chunk, late_in, late_out, late_sem):
            copy.start()

    start_early(0)
    start_late(0)

    barrier = pltpu.get_barrier_semaphore()

    def line_id(ahead):
        return {"depth": lax.rem(me + ahead, n)}

    def group_id(ahead):
        other = lax.rem(place + ahead, group)
        return {"row": other // col_size, "col": lax.rem(other, col_size)}

    def chip_id(ahead):
        other = lax.rem(chip + ahead, chips)
        return {"row": other // per_row, "col": 2 * lax.rem(other, per_row) + core}

    for ahead in range(1, n):
        pl.semaphore_signal(barrier, inc=1, device_id=line_id(ahead), device_id_type=MESH)
    for ahead in range(1, group):
        pl.semaphore_signal(barrier, inc=1, device_id=group_id(ahead), device_id_type=MESH)
    pl.semaphore_wait(barrier, n - 1 + group - 1)

    proj[...] = jnp.zeros_like(proj)
    norm[...] = jnp.zeros_like(norm)
    load_grad.wait()
    load_hidden.wait()

    def right_copy(chunk, kind, half):
        slot = lax.rem(chunk, SLOTS)
        return pltpu.make_async_remote_copy(
            src_ref=to_right.at[slot, kind, half],
            dst_ref=from_left.at[chunk, kind, half],
            send_sem=send_right_sem.at[slot, kind, half],
            recv_sem=recv_left_sem.at[chunk, kind, half],
            device_id={"depth": right},
            device_id_type=MESH,
        )

    def left_copy(chunk, kind, half):
        slot = lax.rem(chunk, SLOTS)
        return pltpu.make_async_remote_copy(
            src_ref=to_left.at[slot, kind, half],
            dst_ref=from_right.at[chunk, kind, half],
            send_sem=send_left_sem.at[slot, kind, half],
            recv_sem=recv_right_sem.at[chunk, kind, half],
            device_id={"depth": left},
            device_id_type=MESH,
        )

    def pass_on(chunk, kind, half, copy, incoming, outgoing, has_source, has_target):
        slot = lax.rem(chunk, SLOTS)

        @pl.when(has_source)
        def _():
            copy(chunk, kind, half).wait_recv()

        @pl.when(has_target)
        def _():
            @pl.when(chunk >= SLOTS)
            def _():
                copy(chunk - SLOTS, kind, half).wait_send()

            @pl.when(has_source)
            def _():
                outgoing[slot, kind, half] = (
                    own[lax.rem(chunk, ring), kind, half] + incoming[chunk, kind, half].astype(jnp.float32)
                ).astype(jnp.bfloat16)

            @pl.when(jnp.logical_not(has_source))
            def _():
                outgoing[slot, kind, half] = own[lax.rem(chunk, ring), kind, half].astype(jnp.bfloat16)

            copy(chunk, kind, half).start()

    def result_copies(chunk):
        slot = lax.rem(chunk, 2)
        return (
            pltpu.make_async_copy(
                result.at[slot, 0], active_hbm.at[:, columns(chunk)], result_sem.at[slot, 0]
            ),
            pltpu.make_async_copy(
                result.at[slot, 1], pre_grad_hbm.at[:, columns(chunk)], result_sem.at[slot, 1]
            ),
        )

    @pl.loop(0, chunks + tail)
    def _(step):
        @pl.when(step < chunks)
        def _():
            @pl.when(step + 1 < chunks)
            def _():
                start_early(step + 1)

            for copy in weight_loads(step, early_in, early_out, early_sem):
                copy.wait()
            slot = lax.rem(step, 2)
            for half in range(HALVES):
                own[lax.rem(step, ring), 0, half] = contract_cols(
                    grad[half * sub : (half + 1) * sub, :], early_out[slot]
                )
            for half in range(HALVES):
                own[lax.rem(step, ring), 1, half] = jnp.dot(
                    hidden[half * sub : (half + 1) * sub, :],
                    early_in[slot],
                    preferred_element_type=jnp.float32,
                )

        going_right = step - LAG * me
        going_left = step - LAG * (n - 1 - me)
        for kind in range(2):
            for half in range(HALVES):

                @pl.when(jnp.logical_and(going_right >= 0, going_right < chunks))
                def _():
                    pass_on(
                        going_right, kind, half, right_copy, from_left, to_right, has_left, has_right
                    )

                @pl.when(jnp.logical_and(going_left >= 0, going_left < chunks))
                def _():
                    pass_on(
                        going_left, kind, half, left_copy, from_right, to_left, has_right, has_left
                    )

        done = step - tail

        @pl.when(done >= 0)
        def _():
            slot = lax.rem(done, 2)

            @pl.when(done + 1 < chunks)
            def _():
                start_late(done + 1)

            @pl.when(done >= 2)
            def _():
                for copy in result_copies(done - 2):
                    copy.wait()

            for kind in range(2):
                for half in range(HALVES):

                    @pl.when(has_left)
                    def _():
                        own[lax.rem(done, ring), kind, half] += from_left[done, kind, half].astype(jnp.float32)

                    @pl.when(has_right)
                    def _():
                        own[lax.rem(done, ring), kind, half] += from_right[done, kind, half].astype(jnp.float32)

            bias = b_in[:, columns(done)]
            bias_grad = jnp.zeros((1, CHUNK), jnp.float32)
            for half in range(HALVES):
                active, pre_grad = gelu_both(own[lax.rem(done, ring), 1, half] + bias, own[lax.rem(done, ring), 0, half])
                pre_grad = pre_grad.astype(jnp.bfloat16)
                result[slot, 0, half * sub : (half + 1) * sub, :] = active.astype(jnp.bfloat16)
                result[slot, 1, half * sub : (half + 1) * sub, :] = pre_grad
                bias_grad += jnp.sum(pre_grad.astype(jnp.float32), axis=0, keepdims=True)
            bias_ref[:, columns(done)] = bias_grad
            for copy in result_copies(done):
                copy.start()
            for copy in weight_loads(done, late_in, late_out, late_sem):
                copy.wait()

            block = width // 2
            for part in range(2):
                span = slice(part * block, (part + 1) * block)
                proj[:, span] += jnp.dot(
                    result[slot, 0], late_out[slot, :, span], preferred_element_type=jnp.float32
                )
            for part in range(2):
                span = slice(part * block, (part + 1) * block)
                norm[:, span] += contract_cols(result[slot, 1], late_in[slot, span, :])

    def remote(src, dst, sems, at, device):
        return pltpu.make_async_remote_copy(
            src_ref=src,
            dst_ref=dst,
            send_sem=sems.at[0, at],
            recv_sem=sems.at[1, at],
            device_id=device,
            device_id_type=MESH,
        )

    bias_send[...] = bias_ref[...]
    bias_copies = [
        remote(bias_send, bias_recv.at[ahead - 1], bias_sems, ahead - 1, line_id(ahead))
        for ahead in range(1, n)
    ]
    for copy in bias_copies:
        copy.start()

    def rows_of(chip_at, core_at):
        at = (chip_at * 2 + core_at) * block_rows
        return pl.ds(pl.multiple_of(at, block_rows), block_rows)

    totals, stages = (norm, proj), (grad, hidden)
    twin_rows = chips * block_rows
    twin_copies = []
    for at in range(2):
        for which in range(chips):
            stages[at][which * block_rows : (which + 1) * block_rows, :] = totals[at][
                rows_of(which, 1 - core), :
            ].astype(jnp.bfloat16)
        copy = remote(
            stages[at].at[:twin_rows],
            twin_recv.at[at],
            twin_sems,
            at,
            {"col": col + 1 - 2 * core},
        )
        copy.start()
        twin_copies.append(copy)

    def both_cores(at, which):
        from_twin = twin_recv[at, pl.ds(pl.multiple_of(which * block_rows, block_rows), block_rows), :]
        return totals[at][rows_of(which, core), :] + from_twin.astype(jnp.float32)

    chip_copies = []
    for at in range(2):
        twin_copies[at].wait_recv()
        of_array = []
        for ahead in range(1, chips):
            spot = slice(twin_rows + (ahead - 1) * block_rows, twin_rows + ahead * block_rows)
            stages[at][spot, :] = both_cores(at, lax.rem(chip + ahead, chips)).astype(jnp.bfloat16)
            copy = remote(
                stages[at].at[spot],
                chip_recv.at[at, ahead - 1],
                chip_sems,
                at * (chips - 1) + ahead - 1,
                chip_id(ahead),
            )
            copy.start()
            of_array.append(copy)
        chip_copies.append(of_array)

    def summed(at):
        value = both_cores(at, chip)
        for ahead in range(1, chips):
            chip_copies[at][ahead - 1].wait_recv()
            value += chip_recv[at, ahead - 1].astype(jnp.float32)
        return value

    mine = pl.ds(0, block_rows)
    norm_grad = summed(0)
    sums_send[0] = jnp.sum(norm_grad * normed[...], axis=0, keepdims=True)
    sums_send[1] = jnp.sum(norm_grad, axis=0, keepdims=True)
    sums_copies = [
        remote(sums_send, sums_recv.at[ahead - 1], sums_sems, ahead - 1, group_id(ahead))
        for ahead in range(1, group)
    ]
    for copy in sums_copies:
        copy.start()
    scaled = norm_grad * ln_gain[...]
    first = jnp.sum(scaled, axis=1, keepdims=True)
    second = jnp.sum(scaled * normed[...], axis=1, keepdims=True)
    lane = lax.broadcasted_iota(jnp.int32, stats_send.shape, 1)
    stats_send[...] = jnp.where(lane == 0, first, second)
    stats_copies = [
        remote(stats_send, stats_recv.at[ahead - 1], stats_sems, ahead - 1, line_id(ahead))
        for ahead in range(1, n)
    ]
    for copy in stats_copies:
        copy.start()
    norm[mine, :] = scaled

    output_ref[...] = (inputs[...].astype(jnp.float32) + (summed(1) + b_out[...])).astype(
        jnp.bfloat16
    )

    stats = stats_send[...]
    for ahead in range(1, n):
        stats_copies[ahead - 1].wait_recv()
        stats += stats_recv[ahead - 1]
    features = n * width
    grad_inputs_ref[...] = (
        cotangent[...].astype(jnp.float32)
        + inv_std[...]
        * (norm[mine, :] - stats[:, :1] / features - normed[...] * (stats[:, 1:2] / features))
    ).astype(jnp.bfloat16)
    sums = sums_send[...]
    for ahead in range(1, group):
        sums_copies[ahead - 1].wait_recv()
        sums += sums_recv[ahead - 1]
    sums_ref[...] = sums
    bias_total = bias_send[...]
    for ahead in range(1, n):
        bias_copies[ahead - 1].wait_recv()
        bias_total += bias_recv[ahead - 1]
    bias_ref[...] = bias_total / n
    for copy in [
        *twin_copies,
        *chip_copies[0],
        *chip_copies[1],
        *stats_copies,
        *sums_copies,
        *bias_copies,
    ]:
        copy.wait_send()
    for chunk in range(max(0, chunks - 2), chunks):
        for copy in result_copies(chunk):
            copy.wait()
    for chunk in range(max(0, chunks - SLOTS), chunks):
        for kind in range(2):
            for half in range(HALVES):

                @pl.when(has_right)
                def _():
                    right_copy(chunk, kind, half).wait_send()

                @pl.when(has_left)
                def _():
                    left_copy(chunk, kind, half).wait_send()


def line_call(
    n, row_size, col_size, hidden_all, grad_all, w_in, w_out, b_in, b_out, ln_gain, inputs, cotangent, normed, inv_std
):
    rows, width = hidden_all.shape
    group = row_size * col_size
    chips = group // 2
    block_rows = rows // group
    local = w_in.shape[1]
    chunks = local // CHUNK
    sub = rows // HALVES
    anywhere = pl.BlockSpec(memory_space=pl.ANY)
    vmem = pl.BlockSpec(memory_space=pltpu.VMEM)
    bf16, f32 = jnp.bfloat16, jnp.float32
    parts = (2, HALVES)
    return pl.pallas_call(
        partial(line_kernel, n, row_size, col_size),
        out_shape=(
            jax.ShapeDtypeStruct((rows, local), bf16),
            jax.ShapeDtypeStruct((rows, local), bf16),
            jax.ShapeDtypeStruct((block_rows, width), bf16),
            jax.ShapeDtypeStruct((block_rows, width), bf16),
            jax.ShapeDtypeStruct((1, local), f32),
            jax.ShapeDtypeStruct((2, 1, width), f32),
        ),
        in_specs=[anywhere] * 4 + [vmem] * 7,
        out_specs=(anywhere,) * 2 + (vmem,) * 4,
        scratch_shapes=[
            pltpu.VMEM((rows, width), bf16),
            pltpu.VMEM((rows, width), bf16),
            pltpu.VMEM((min(chunks, LAG * (n - 1) + 1), *parts, sub, CHUNK), f32),
            pltpu.VMEM((chunks, *parts, sub, CHUNK), bf16),
            pltpu.VMEM((chunks, *parts, sub, CHUNK), bf16),
            pltpu.VMEM((SLOTS, *parts, sub, CHUNK), bf16),
            pltpu.VMEM((SLOTS, *parts, sub, CHUNK), bf16),
            pltpu.VMEM((rows, width), f32),
            pltpu.VMEM((rows, width), f32),
            pltpu.VMEM((2, width, CHUNK), bf16),
            pltpu.VMEM((2, CHUNK, width), bf16),
            pltpu.VMEM((2, width, CHUNK), bf16),
            pltpu.VMEM((2, CHUNK, width), bf16),
            pltpu.VMEM((2, 2, rows, CHUNK), bf16),
            pltpu.SemaphoreType.DMA((2,)),
            pltpu.SemaphoreType.DMA((2, 2)),
            pltpu.SemaphoreType.DMA((2, 2)),
            pltpu.SemaphoreType.DMA((2, 2)),
            pltpu.SemaphoreType.DMA((SLOTS, *parts)),
            pltpu.SemaphoreType.DMA((SLOTS, *parts)),
            pltpu.SemaphoreType.DMA((chunks, *parts)),
            pltpu.SemaphoreType.DMA((chunks, *parts)),
            pltpu.VMEM((2, chips * block_rows, width), bf16),
            pltpu.VMEM((2, chips - 1, block_rows, width), bf16),
            pltpu.VMEM((block_rows, 128), f32),
            pltpu.VMEM((n - 1, block_rows, 128), f32),
            pltpu.VMEM((1, local), f32),
            pltpu.VMEM((n - 1, 1, local), f32),
            pltpu.VMEM((2, 1, width), f32),
            pltpu.VMEM((group - 1, 2, 1, width), f32),
            pltpu.SemaphoreType.DMA((2, 2)),
            pltpu.SemaphoreType.DMA((2, 2 * (chips - 1))),
            pltpu.SemaphoreType.DMA((2, n - 1)),
            pltpu.SemaphoreType.DMA((2, n - 1)),
            pltpu.SemaphoreType.DMA((2, group - 1)),
        ],
        compiler_params=pltpu.CompilerParams(
            collective_id=0, has_side_effects=True, vmem_limit_bytes=62 * 2**20
        ),
        cost_estimate=pl.CostEstimate(
            flops=8 * rows * width * local,
            bytes_accessed=8 * width * local + 12 * rows * width,
            transcendentals=rows * local,
        ),
    )(
        hidden_all, grad_all, w_in, w_out, b_in, b_out, ln_gain, inputs, cotangent, normed, inv_std
    )


def per_device(n, row_size, col_size, inputs, ln_gain, ln_shift, w_in, b_in, w_out, b_out, cotangent):
    width = inputs.shape[1]
    grad_all = lax.all_gather(cotangent, ("row", "col"), axis=0, tiled=True)
    wide_in = inputs.astype(jnp.float32)
    part_mean = jnp.mean(wide_in, axis=1, keepdims=True)
    part_square = jnp.sum((wide_in - part_mean) ** 2, axis=1, keepdims=True)
    stats = lax.all_gather(jnp.concatenate([part_mean, part_square], axis=1), "depth", axis=0)
    row_mean = jnp.mean(stats[:, :, :1], axis=0)
    row_var = (
        jnp.sum(stats[:, :, 1:], axis=0)
        + width * jnp.sum((stats[:, :, :1] - row_mean[None]) ** 2, axis=0)
    ) / (n * width)
    inv_std = 1.0 / jnp.sqrt(row_var + 1e-05)
    normed = (wide_in - row_mean) * inv_std
    hidden_in = (normed * ln_gain + ln_shift).astype(jnp.bfloat16)
    hidden_all = lax.all_gather(hidden_in, ("row", "col"), axis=0, tiled=True)
    active_all, pre_grad_all, output, grad_inputs, grad_b_in, sums = line_call(
        n,
        row_size,
        col_size,
        hidden_all,
        grad_all,
        w_in,
        w_out,
        b_in.reshape(1, -1),
        b_out.reshape(1, -1),
        ln_gain.reshape(1, -1),
        inputs,
        cotangent,
        normed,
        inv_std,
    )
    grad_w_out = contract_rows(active_all, grad_all).astype(jnp.bfloat16)
    grad_w_in = contract_rows(hidden_all, pre_grad_all).astype(jnp.bfloat16)
    grad_b_out = jnp.sum(grad_all.astype(jnp.float32), axis=0)
    grad_gain, grad_shift = sums[0, 0], sums[1, 0]
    grad_b_in = grad_b_in[0]
    return (
        output,
        grad_inputs,
        grad_w_in,
        grad_b_in,
        grad_w_out,
        grad_b_out,
        grad_gain,
        grad_shift,
    )


def solution(mesh):
    return jax.shard_map(
        partial(per_device, mesh.shape["depth"], mesh.shape["row"], mesh.shape["col"]),
        mesh=mesh,
        in_specs=(
            P(("row", "col"), "depth"),
            P("depth"),
            P("depth"),
            P("depth", ("row", "col")),
            P(("row", "col")),
            P(("row", "col"), "depth"),
            P("depth"),
            P(("row", "col"), "depth"),
        ),
        out_specs=(
            P(("row", "col"), "depth"),
            P(("row", "col"), "depth"),
            P("depth", ("row", "col")),
            P(("row", "col")),
            P(("row", "col"), "depth"),
            P("depth"),
            P("depth"),
            P("depth"),
        ),
        check_vma=False,
    )
```
